256 devices in a mesh: node: 16 (over z, core), fsdp: 16 (over x, y).
Axes of the slice: x: 4, y: 4, z: 8, core: 2. Of those that a mesh axis runs over, the one named last changes fastest.
Arguments:
- hidden: bfloat16 [32768, 8192], P(('node', 'fsdp')), may hold values from -6 to 6
- queries: bfloat16 [32768, 4096], P(('node', 'fsdp')), may hold values from -70 to 70
- key_matrix: bfloat16 [8192, 512], P('fsdp'), may hold values from -0.0625 to 0.0625
- value_matrix: bfloat16 [8192, 512], P('fsdp'), may hold values from -0.0625 to 0.0625
- out_weight: bfloat16 [4096, 8192], P('fsdp'), may hold values from -0.25 to 0.25
- lengths: int32 [16, 8], P('node'), may hold values from 1 to 512, 2048 in all within a row
Outputs:
- updated: float32 [32768, 8192], P(('node', 'fsdp'))
The draws below stay inside these ranges and needn't reach their ends.
All inputs are finite; a program needn't handle non-finite values.
Results may differ from the reference program's by a relative error of at most 0.0095.
Values may be sent and summed in bfloat16 or wider, within the bound.
A program may use at most 128 MiB of HBM per device.

```python
import math
import jax
import jax.numpy as jnp
import numpy as np
from jax import lax

MODEL_WIDTH = 8192
HEAD_WIDTH = 128
QUERY_HEADS = 32
KEY_VALUE_HEADS = 4
NSEG = 8
ROW_TOKENS = 2048
TOKENS = 32768
MAXLEN = 512
N_NODE = 16


def draw_queries(key, part):
    key = jax.random.fold_in(key, 7)
    rows = N_NODE * ROW_TOKENS
    shape = (rows, QUERY_HEADS * HEAD_WIDTH)
    value_rows = jnp.clip(jax.random.normal(key, shape, jnp.float32), -6.0, 6.0)
    return value_rows.astype(jnp.bfloat16)


def shard_levels(key, shape, shards, low, top_value):
    level, own = 1.0, jax.random.fold_in(key, 6)
    for position, blocks in shards:
        heights = jnp.exp(jax.random.uniform(jax.random.fold_in(own, position), (blocks,), jnp.float32, low / len(shards), top_value / len(shards)))
        level = level * jnp.repeat(heights, shape[position] // blocks).reshape([-1 if axis == position else 1 for axis in range(len(shape))])
    return level


def length_profile(count, total, most, lean):
    loads = [(1 << 20) // math.isqrt(standing ** lean) + 1 for standing in range(2, count + 1)]
    surplus, holding = total - most - (count - 1), [1] * (count - 1)
    while surplus > 0:
        candidates = [i for i in range(count - 1) if holding[i] < most]
        mass, remaining = sum([loads[i] for i in candidates]), surplus
        for i in candidates:
            extra = min(most - holding[i], max(1, remaining * loads[i] // mass), surplus)
            holding[i] = holding[i] + extra
            surplus = surplus - extra
    return np.array([most] + holding)


def ragged_sizes(own_key, amount, total, most, lean):
    if amount == 2:
        one = jax.random.randint(own_key, (), max(1, total - most), min(most, total - 1) + 1)
        return jnp.stack([one, total - one])
    tallies = jnp.asarray(length_profile(amount, total, most, lean), jnp.int32)
    twos = (amount - 1) // 2
    source_of, taker = tallies[1:1 + 2 * twos:2], tallies[2:2 + 2 * twos:2]
    slack = jnp.minimum(source_of - 1, most - taker)
    passed = jax.random.randint(jax.random.fold_in(own_key, 1), (twos,), 0, 1 << 20) % (slack + 1)
    tallies = tallies.at[1:1 + 2 * twos:2].set(source_of - passed).at[2:2 + 2 * twos:2].set(taker + passed)
    return tallies[jax.random.permutation(jax.random.fold_in(own_key, 2), amount)]


def centred(stream_key, shape, scale, limit, shards=(), kind=jnp.bfloat16):
    drawn = jax.random.normal(stream_key, shape, jnp.float32) * scale
    if len(shards) > 0:
        drawn = shard_levels(stream_key, shape, shards, -0.22, 0.18) * drawn
    return jnp.clip(drawn, min=-limit, max=limit).astype(kind)


def setup_inputs(seed: int = 0) -> dict:
    keys = jax.random.split(jax.random.key(seed), 7)
    return {
        "hidden": centred(keys[0], (TOKENS, MODEL_WIDTH), 1.0, 6.0, ((0, 256),)),
        "queries": draw_queries(jax.random.fold_in(keys[6], 71), 0),
        "key_matrix": centred(keys[2], (MODEL_WIDTH, KEY_VALUE_HEADS * HEAD_WIDTH), MODEL_WIDTH ** -0.5, 0.0625, ((0, 16),)),
        "value_matrix": centred(keys[3], (MODEL_WIDTH, KEY_VALUE_HEADS * HEAD_WIDTH), MODEL_WIDTH ** -0.5, 0.0625, ((0, 16),)),
        "out_weight": centred(keys[4], (QUERY_HEADS * HEAD_WIDTH, MODEL_WIDTH), (QUERY_HEADS * HEAD_WIDTH // 8) ** -0.5, 0.25, ((0, 16),)),
        "lengths": jax.vmap(lambda own: ragged_sizes(own, NSEG, ROW_TOKENS, MAXLEN, 2))(jax.random.split(keys[5], N_NODE)).reshape((N_NODE, NSEG)).astype(jnp.int32),
    }


def segment_of(lens, positions):
    ends = jnp.cumsum(lens.astype(jnp.int32))
    return lax.optimization_barrier(jnp.sum((positions[:, None] >= ends[None, :]).astype(jnp.int32), axis=1))

def normalize(hidden_row):
    hidden32 = hidden_row.astype(jnp.float32)
    scale_row = lax.rsqrt(lax.optimization_barrier(jnp.mean(hidden32 * hidden32, axis=1, keepdims=True)) + 1e-05)
    return (hidden32 * scale_row).astype(jnp.bfloat16)

def attend_row(normed, row_of_query, lens, key_matrix, value_matrix):
    key_rows = jnp.dot(normed, key_matrix, preferred_element_type=jnp.float32).astype(jnp.bfloat16)
    value_rows = jnp.dot(normed, value_matrix, preferred_element_type=jnp.float32).astype(jnp.bfloat16)
    positions = jnp.arange(ROW_TOKENS, dtype=jnp.int32)
    seg = segment_of(lens, positions)
    allowed = (positions[None, :] <= positions[:, None]) & (seg[None, :] == seg[:, None])
    query_group = QUERY_HEADS // KEY_VALUE_HEADS
    heads_of_query = row_of_query.reshape(ROW_TOKENS, KEY_VALUE_HEADS, query_group, HEAD_WIDTH).transpose(1, 0, 2, 3)
    heads_of_key = key_rows.reshape(ROW_TOKENS, KEY_VALUE_HEADS, HEAD_WIDTH).transpose(1, 0, 2)
    heads_of_value = value_rows.reshape(ROW_TOKENS, KEY_VALUE_HEADS, HEAD_WIDTH).transpose(1, 0, 2)

    def per_head(items):
        qh, kh, vh = items
        scores = jnp.einsum('tgd,sd->gts', qh.astype(jnp.float32), kh.astype(jnp.float32)) / jnp.sqrt(jnp.float32(HEAD_WIDTH))
        scores = jnp.where(allowed[None], scores, jnp.float32(-1e+30))
        top = lax.optimization_barrier(jnp.max(scores, axis=2, keepdims=True))
        weights = jnp.where(allowed[None], jnp.exp(scores - top), jnp.float32(0.0))
        total = lax.optimization_barrier(jnp.sum(weights, axis=2, keepdims=True))
        rounded = weights.astype(jnp.bfloat16)
        mixed = jnp.einsum('gts,sd->tgd', rounded.astype(jnp.float32), vh.astype(jnp.float32))
        return mixed / jnp.transpose(total, (1, 0, 2))
    outs = lax.map(per_head, (heads_of_query, heads_of_key, heads_of_value))
    return outs.transpose(1, 0, 2, 3).reshape(ROW_TOKENS, QUERY_HEADS * HEAD_WIDTH).astype(jnp.bfloat16)

def reference(hidden, queries, key_matrix, value_matrix, out_weight, lengths):

    def row_fn(packed):
        hidden_row, row_of_query, lens = packed
        normed = normalize(hidden_row)
        attention = attend_row(normed, row_of_query, lens, key_matrix, value_matrix)
        projected = jnp.dot(attention, out_weight, preferred_element_type=jnp.float32)
        return hidden_row.astype(jnp.float32) + projected
    updated = lax.map(row_fn, (hidden.reshape(N_NODE, ROW_TOKENS, MODEL_WIDTH), queries.reshape(N_NODE, ROW_TOKENS, QUERY_HEADS * HEAD_WIDTH), lengths))
    return updated.reshape(TOKENS, MODEL_WIDTH)
```

```python
import jax
import jax.numpy as jnp
from jax import lax
from jax.experimental import pallas as pl
from jax.experimental.pallas import tpu as pltpu
from jax.sharding import PartitionSpec as P

MESH = pl.DeviceIdType.MESH
HEAD = 128
TOK = 128
SLOTS = 8
COLS = 256
F32 = jnp.float32
BF16 = jnp.bfloat16


def gather_copies(buf, ssem, rsem, place, peers):
    x, y = place
    to_x, to_y = peers

    def copy(index, ref, device):
        return pltpu.make_async_remote_copy(
            src_ref=ref, dst_ref=ref, send_sem=ssem.at[index], recv_sem=rsem.at[index],
            device_id=device, device_id_type=MESH,
        )

    xr, xl = lax.rem(x + 1, 4), lax.rem(x + 3, 4)
    yr, yl = lax.rem(y + 1, 4), lax.rem(y + 3, 4)
    first = [copy(k, buf.at[x, 0, y], to_x[k]) for k in range(3)]
    first += [copy(3 + k, buf.at[x, 1, y], to_y[k]) for k in range(3)]
    second = [copy(6 + k, buf.at[:, 0, y], to_y[k]) for k in range(2)]
    second += [copy(8 + k, buf.at[x, 1], to_x[k]) for k in range(2)]
    third = [
        copy(10, buf.at[pl.ds(0, 2), 0, yl], to_y[0]),
        copy(11, buf.at[pl.ds(2, 2), 0, yr], to_y[1]),
        copy(12, buf.at[xl, 1, pl.ds(0, 2)], to_x[0]),
        copy(13, buf.at[xr, 1, pl.ds(2, 2)], to_x[1]),
    ]
    return first, second, third


def kernel(
    lengths, hidden, queries, key_w, value_w, out_w, result,
    xn, xb, kvw, part, part_in, win, qb, lo, wb, at, ob, acc, rb,
    kv_s, kv_r, wo_s, wo_r, sh_s, sh_r, x_s, x_r, q_s, q_r, p_s, p_r,
    win_s, win_r, at_s, at_r, ob_s, ob_r, loc,
):
    node, f = lax.axis_index("node"), lax.axis_index("fsdp")
    z, c = node // 2, lax.rem(node, 2)
    x, y = f // 4, lax.rem(f, 4)
    odd = lax.rem(z, 2)
    other = 1 - c
    half = odd
    pz = z + 1 - 2 * odd
    sz = lax.rem(z + 7 + 2 * odd, 8)
    band = lax.rem((z + 1) // 2, 2)
    sibling = (z * 2 + other, f)
    partner = (pz * 2 + c, f)
    cross = (pz * 2 + other, f)
    sharer = (sz * 2 + c, f)
    to_x = [(node, lax.rem(x + d, 4) * 4 + y) for d in (1, 3, 2)]
    to_y = [(node, x * 4 + lax.rem(y + d, 4)) for d in (1, 3, 2)]
    ahead = [(node, lax.rem(f + k, 16)) for k in range(1, 5)]
    behind = [(node, lax.rem(f + 16 - k, 16)) for k in range(1, 5)]
    place, peers = (x, y), (to_x, to_y)

    def remote(src, dst, ssem, rsem, device):
        return pltpu.make_async_remote_copy(
            src_ref=src, dst_ref=dst, send_sem=ssem, recv_sem=rsem, device_id=device, device_id_type=MESH
        )

    def start(copies):
        for copy in copies:
            copy.start()

    def arrive(copies):
        for copy in copies:
            copy.wait_recv()

    def sent(copies):
        for copy in copies:
            copy.wait_send()

    def chunk(s):
        if s == 0:
            return odd
        if s == SLOTS - 1:
            return 1 - odd
        return s + 1

    def band_col(s):
        return pl.multiple_of((band * 2 + c) * (SLOTS * COLS) + chunk(s) * COLS, COLS)

    local_kv = [
        pltpu.make_async_copy(
            w.at[pl.ds(half * 2, 2), :, pl.ds(pl.multiple_of(c * 256, 256), 256)],
            kvw.at[x, :, y, :, pl.ds(256 * i, 256)],
            loc.at[i],
        )
        for i, w in enumerate((key_w, value_w))
    ]
    start(local_kv)
    local_wo = [
        pltpu.make_async_copy(out_w.at[:, :, pl.ds(band_col(s), COLS)], wb.at[s, x, :, y], loc.at[2 + s])
        for s in range(SLOTS - 1)
    ]
    start(local_wo)
    local_q = pltpu.make_async_copy(
        queries.at[:, pl.ds(pl.multiple_of(c * 2048, 2048), 2048)], qb.at[c], loc.at[9]
    )
    local_q.start()

    barrier = pltpu.get_barrier_semaphore()
    greeted = [sibling, partner, cross, sharer] + to_x + to_y + ahead + behind
    for device in greeted:
        pl.semaphore_signal(barrier, inc=1, device_id=device, device_id_type=MESH)
    pl.semaphore_wait(barrier, len(greeted))

    kv1, kv2, kv3 = gather_copies(kvw, kv_s, kv_r, place, peers)
    wo = [gather_copies(wb.at[s], wo_s.at[s], wo_r.at[s], place, peers) for s in range(SLOTS - 1)]
    share = remote(wb.at[0], wb.at[SLOTS - 1], sh_s, sh_r, sharer)

    for copy in local_kv:
        copy.wait()
    start(kv1)
    send_q = remote(
        queries.at[:, pl.ds(pl.multiple_of(other * 2048, 2048), 2048)], qb.at[c], q_s.at[0], q_r.at[0], sibling
    )
    send_q.start()

    pos = f * TOK + lax.broadcasted_iota(jnp.int32, (TOK, 128), 0)
    end = jnp.int32(0)
    first = jnp.zeros((TOK, 128), jnp.int32)
    for e in range(8):
        end = end + lengths[0, e]
        first = jnp.where(pos >= end, end, first)
    lo[c] = (first - f * TOK + 4 * TOK).astype(F32)
    send_lo = remote(lo.at[c], lo.at[c], q_s.at[1], q_r.at[1], sibling)
    send_lo.start()

    @pl.loop(0, TOK // 16)
    def _(block):
        rows = pl.ds(pl.multiple_of(block * 16, 16), 16)
        h32 = hidden[rows, :].astype(F32)
        scale = lax.rsqrt(jnp.sum(h32 * h32, axis=1, keepdims=True) * (1.0 / 8192.0) + 1e-05)
        normed = (h32 * scale).astype(BF16)
        for fx in range(4):
            for fy in range(4):
                for hf in range(2):
                    for colour in range(2):
                        src = (fx * 4 + fy) * 512 + hf * 256 + colour * 128
                        dst = ((fx * 2 + colour) * 4 + fy) * 128
                        xn[hf, rows, pl.ds(dst, 128)] = normed[:, src:src + 128]

    send_x = [
        remote(xn.at[1 - half], xb.at[2 + c], x_s.at[0], x_r.at[0], partner),
        remote(xn.at[half], xb.at[c], x_s.at[1], x_r.at[1], sibling),
    ]
    start(send_x)
    local_x = pltpu.make_async_copy(xn.at[half], xb.at[c], loc.at[10])
    local_x.start()

    def wo_first(s):
        local_wo[s].wait()
        start(wo[s][0])

    def wo_second(s):
        arrive(wo[s][0])
        start(wo[s][1])

    def wo_third(s):
        arrive(wo[s][1])
        start(wo[s][2])

    def wo_done(s):
        arrive(wo[s][2])

    arrive(kv1)
    start(kv2)
    for s in range(3):
        wo_first(s)
    arrive(kv2)
    start(kv3)
    for s in range(3, SLOTS - 1):
        wo_first(s)
    send_x[0].wait_recv()
    pass_x = remote(xb.at[2 + c], xb.at[2 + c], x_s.at[2], x_r.at[2], sibling)
    pass_x.start()
    wo_second(0)
    arrive(kv3)
    wo_second(1)
    send_x[1].wait_recv()
    pass_x.wait_recv()
    local_x.wait()

    part[...] = jnp.zeros_like(part)

    @pl.loop(0, 4)
    def _(fx):
        w = kvw[fx].reshape(1024, 512)
        feats = pl.ds(pl.multiple_of(fx * 1024, 1024), 1024)
        for t in range(4):
            part[t] += jnp.dot(xb[t, :, feats], w, preferred_element_type=F32)

    send_p = remote(part.at[pl.ds(2, 2)], part_in, p_s.at[0], p_r.at[0], partner)
    send_p.start()
    wo_third(0)
    wo_second(2)
    send_p.wait_recv()
    for r in range(2):
        win[r, 4] = (part[r] + part_in[r]).astype(BF16)
    send_win = [
        remote(win.at[:, 4], win.at[:, 4 - k], win_s.at[k - 1], win_r.at[k - 1], ahead[k - 1]) for k in range(1, 5)
    ]
    start(send_win)
    wo_third(1)
    wo_second(3)
    local_q.wait()
    send_q.wait_recv()
    send_lo.wait_recv()
    arrive(send_win)

    col = lax.broadcasted_iota(jnp.int32, (TOK, 5 * TOK), 1)
    row = lax.broadcasted_iota(jnp.int32, (TOK, 5 * TOK), 0)

    def attend(j):
        @pl.loop(0, 8)
        def _(step):
            r, pair = step // 4, lax.rem(step, 4)
            both = qb[r, :, pl.ds(pl.multiple_of(j * 1024 + pair * 256, 256), 256)]
            q = jnp.concatenate([both[:, :HEAD], both[:, HEAD:]], axis=0)
            k = win[r, :, :, pl.ds(j * HEAD, HEAD)].reshape(5 * TOK, HEAD)
            v = win[r, :, :, pl.ds(256 + j * HEAD, HEAD)].reshape(5 * TOK, HEAD)
            allowed = ((col.astype(F32) >= lo[r][:, :1]) & (col <= row + 4 * TOK))[None]
            s = lax.dot_general(q, k, (((1,), (1,)), ((), ())), preferred_element_type=F32)
            s = (s * (HEAD ** -0.5)).reshape(2, TOK, 5 * TOK)
            s = jnp.where(allowed, s, F32(-1e30))
            top = jnp.max(s, axis=2, keepdims=True)
            w = jnp.where(allowed, jnp.exp(s - top), F32(0.0))
            total = jnp.sum(w, axis=2, keepdims=True)
            mixed = jnp.dot(w.astype(BF16).reshape(2 * TOK, 5 * TOK), v, preferred_element_type=F32)
            mixed = (mixed.reshape(2, TOK, HEAD) / total).astype(BF16)
            at[2 * c + j, r, :, pl.ds(pl.multiple_of(pair * HEAD, HEAD), HEAD)] = mixed[0]
            at[2 * c + j, r, :, pl.ds(pl.multiple_of((4 + pair) * HEAD, HEAD), HEAD)] = mixed[1]

        mine = at.at[2 * c + j, pl.ds(0, 2)]
        theirs = at.at[2 * c + j, pl.ds(2, 2)]
        copies = [
            remote(mine, theirs, at_s.at[3 * j], at_r.at[3 * j], partner),
            remote(mine, mine, at_s.at[3 * j + 1], at_r.at[3 * j + 1], sibling),
            remote(theirs, theirs, at_s.at[3 * j + 2], at_r.at[3 * j + 2], sibling),
        ]
        start(copies[:2])
        return copies

    def pass_on(copies):
        copies[0].wait_recv()
        copies[2].start()

    heads0 = attend(0)
    wo_third(2)
    wo_second(4)
    wo_done(0)
    share.start()
    heads1 = attend(1)
    wo_third(3)
    wo_second(5)
    pass_on(heads0)
    wo_third(4)
    wo_second(6)
    pass_on(heads1)
    for copies in (heads0, heads1):
        copies[1].wait_recv()
        copies[2].wait_recv()

    outs = []

    def project(s):
        acc[...] = jnp.zeros_like(acc)

        @pl.loop(0, 4)
        def _(g):
            acc[...] += jnp.dot(
                at[g].reshape(4 * TOK, 1024), wb[s, g].reshape(1024, COLS), preferred_element_type=F32
            )

        ob[s] = acc[...].astype(BF16).reshape(4, TOK, COLS)
        cols = pl.ds(band_col(s), COLS)
        rb[:, cols] = ob[s, c]
        copies = [
            remote(ob.at[s, slot], rb.at[:, cols], ob_s.at[s, i], ob_r.at[s, i], device)
            for i, (slot, device) in enumerate(((2 + c, partner), (2 + other, cross), (other, sibling)))
        ]
        start(copies)
        outs.extend(copies)

    project(0)
    wo_done(1)
    project(1)
    wo_third(5)
    wo_done(2)
    project(2)
    wo_done(3)
    project(3)
    wo_third(6)
    wo_done(4)
    project(4)
    wo_done(5)
    project(5)
    share.wait_recv()
    project(7)
    wo_done(6)
    project(6)
    arrive(outs)
    write = pltpu.make_async_copy(rb, result, loc.at[11])
    write.start()

    sent(kv1 + kv2 + kv3 + send_x + [pass_x, send_q, send_lo, send_p, share] + send_win + heads0 + heads1 + outs)
    for s in range(SLOTS - 1):
        for copies in wo[s]:
            sent(copies)
    write.wait()


def body(hidden, queries, key_matrix, value_matrix, out_weight, lengths):
    dma = pltpu.SemaphoreType.DMA
    vmem, anywhere = pl.BlockSpec(memory_space=pltpu.VMEM), pl.BlockSpec(memory_space=pl.ANY)
    projected = pl.pallas_call(
        kernel,
        out_shape=jax.ShapeDtypeStruct((TOK, 8192), BF16),
        in_specs=[pl.BlockSpec(memory_space=pltpu.SMEM), vmem] + [anywhere] * 4,
        out_specs=anywhere,
        scratch_shapes=[
            pltpu.VMEM((2, TOK, 4096), BF16),
            pltpu.VMEM((4, TOK, 4096), BF16),
            pltpu.VMEM((4, 2, 4, 128, 512), BF16),
            pltpu.VMEM((4, TOK, 512), F32),
            pltpu.VMEM((2, TOK, 512), F32),
            pltpu.VMEM((2, 5, TOK, 512), BF16),
            pltpu.VMEM((2, TOK, 2048), BF16),
            pltpu.VMEM((2, TOK, 128), F32),
            pltpu.VMEM((SLOTS, 4, 2, 4, 128, COLS), BF16),
            pltpu.VMEM((4, 4, TOK, 1024), BF16),
            pltpu.VMEM((SLOTS, 4, TOK, COLS), BF16),
            pltpu.VMEM((4 * TOK, COLS), F32),
            pltpu.VMEM((TOK, 8192), BF16),
            dma((14,)), dma((14,)),
            dma((SLOTS - 1, 14)), dma((SLOTS - 1, 14)),
            dma, dma,
            dma((3,)), dma((3,)),
            dma((2,)), dma((2,)),
            dma((1,)), dma((1,)),
            dma((4,)), dma((4,)),
            dma((6,)), dma((6,)),
            dma((SLOTS, 3)), dma((SLOTS, 3)),
            dma((12,)),
        ],
        compiler_params=pltpu.CompilerParams(
            collective_id=0, has_side_effects=True, vmem_limit_bytes=60 * 2 ** 20
        ),
        cost_estimate=pl.CostEstimate(flops=12 * 10 ** 9, bytes_accessed=16 * 2 ** 20, transcendentals=3 * 10 ** 6),
    )(
        lengths, hidden, queries,
        key_matrix.reshape(4, 128, 512), value_matrix.reshape(4, 128, 512), out_weight.reshape(2, 128, 8192),
    )
    return hidden.astype(F32) + projected.astype(F32)


def solution(mesh):
    placed = (
        P(("node", "fsdp"), None),
        P(("node", "fsdp"), None),
        P("fsdp", None),
        P("fsdp", None),
        P("fsdp", None),
        P("node", None),
    )
    return jax.shard_map(
        body, mesh=mesh, in_specs=placed, out_specs=P(("node", "fsdp"), None), check_vma=False
    )
```

```python
import jax
import jax.numpy as jnp
from jax import lax
from jax.experimental import pallas as pl
from jax.experimental.pallas import tpu as pltpu
from jax.sharding import PartitionSpec as P

MESH = pl.DeviceIdType.MESH
HEAD = 128
TOK = 128
SLOTS = 8
COLS = 256
F32 = jnp.float32
BF16 = jnp.bfloat16


def gather_copies(piece, ssem, rsem, place, peers):
    x, y = place
    to_x, to_y = peers

    def copy(index, ref, device):
        return pltpu.make_async_remote_copy(
            src_ref=ref, dst_ref=ref, send_sem=ssem.at[index], recv_sem=rsem.at[index],
            device_id=device, device_id_type=MESH,
        )

    xr, xl = lax.rem(x + 1, 4), lax.rem(x + 3, 4)
    yr, yl = lax.rem(y + 1, 4), lax.rem(y + 3, 4)
    every, low, high = slice(None), pl.ds(0, 2), pl.ds(2, 2)
    first = [copy(k, piece(x, 0, y), to_x[k]) for k in range(3)]
    first += [copy(3 + k, piece(x, 1, y), to_y[k]) for k in range(3)]
    second = [copy(6 + k, piece(every, 0, y), to_y[k]) for k in range(2)]
    second += [copy(8 + k, piece(x, 1, every), to_x[k]) for k in range(2)]
    third = [
        copy(10, piece(low, 0, yl), to_y[0]),
        copy(11, piece(high, 0, yr), to_y[1]),
        copy(12, piece(xl, 1, low), to_x[0]),
        copy(13, piece(xr, 1, high), to_x[1]),
    ]
    return first, second, third


def kernel(
    lengths, hidden, queries, key_w, value_w, out_w, result,
    xn, xo, xz, kvw, part, part_z, part_in, win, qb, lo, wb, at, ob, acc, rb,
    kv_s, kv_r, wo_s, wo_r, sh_s, sh_r, x_s, x_r, q_s, q_r, p_s, p_r,
    win_s, win_r, at_s, at_r, ob_s, ob_r, loc,
):
    node, f = lax.axis_index("node"), lax.axis_index("fsdp")
    z, c = node // 2, lax.rem(node, 2)
    x, y = f // 4, lax.rem(f, 4)
    odd = lax.rem(z, 2)
    other = 1 - c
    pz = z + 1 - 2 * odd
    sz = lax.rem(z + 7 + 2 * odd, 8)
    band = lax.rem((z + 1) // 2, 2)
    sibling = (z * 2 + other, f)
    partner = (pz * 2 + c, f)
    cross = (pz * 2 + other, f)
    sharer = (sz * 2 + c, f)
    to_x = [(node, lax.rem(x + d, 4) * 4 + y) for d in (1, 3, 2)]
    to_y = [(node, x * 4 + lax.rem(y + d, 4)) for d in (1, 3, 2)]
    place, peers = (x, y), (to_x, to_y)

    def remote(src, dst, ssem, rsem, device):
        return pltpu.make_async_remote_copy(
            src_ref=src, dst_ref=dst, send_sem=ssem, recv_sem=rsem, device_id=device, device_id_type=MESH
        )

    flying, landed = [], set()

    def start(copies):
        for copy in copies:
            copy.start()
            flying.append(copy)

    def arrive(copies):
        for copy in copies:
            copy.wait_recv()
            landed.add(id(copy))

    def finish():
        for copy in flying:
            if id(copy) not in landed:
                copy.wait_recv()
        for copy in flying:
            copy.wait_send()

    def chunk(s):
        if s == 0:
            return odd
        if s == SLOTS - 1:
            return 1 - odd
        return s + 1

    def band_col(s):
        return pl.multiple_of((band * 2 + c) * (SLOTS * COLS) + chunk(s) * COLS, COLS)

    local_kv = [
        pltpu.make_async_copy(
            w.at[:, odd, :, pl.ds(pl.multiple_of(c * 256, 256), 256)],
            kvw.at[:, x, y, :, pl.ds(256 * i, 256)],
            loc.at[i],
        )
        for i, w in enumerate((key_w, value_w))
    ]
    for copy in local_kv:
        copy.start()
    local_wo = [
        pltpu.make_async_copy(out_w.at[:, :, pl.ds(band_col(s), COLS)], wb.at[s, x, :, y], loc.at[2 + s])
        for s in range(SLOTS - 1)
    ]
    for copy in local_wo:
        copy.start()
    local_q = pltpu.make_async_copy(
        queries.at[:, pl.ds(pl.multiple_of(c * 2048, 2048), 2048)], qb.at[c], loc.at[9]
    )
    local_q.start()

    barrier = pltpu.get_barrier_semaphore()
    greeted = [sibling, partner, cross, sharer] + to_x + to_y
    for device in greeted:
        pl.semaphore_signal(barrier, inc=1, device_id=device, device_id_type=MESH)
    pl.semaphore_wait(barrier, len(greeted))

    kv1, kv2, kv3 = gather_copies(lambda i, colour, k: kvw.at[colour, i, k], kv_s, kv_r, place, peers)
    wo = [
        gather_copies(lambda i, colour, k, s=s: wb.at[s, i, colour, k], wo_s.at[s], wo_r.at[s], place, peers)
        for s in range(SLOTS - 1)
    ]
    share = remote(wb.at[0], wb.at[SLOTS - 1], sh_s, sh_r, sharer)

    for copy in local_kv:
        copy.wait()
    start(kv1)
    send_q = remote(
        queries.at[:, pl.ds(pl.multiple_of(other * 2048, 2048), 2048)], qb.at[c], q_s.at[0], q_r.at[0], sibling
    )
    start([send_q])

    pos = f * TOK + lax.broadcasted_iota(jnp.int32, (TOK, 128), 0)
    end = jnp.int32(0)
    first = jnp.zeros((TOK, 128), jnp.int32)
    for e in range(8):
        end = end + lengths[0, e]
        first = jnp.where(pos >= end, end, first)
    lo[c] = (first - f * TOK + 4 * TOK).astype(F32)
    send_lo = remote(lo.at[c], lo.at[c], q_s.at[1], q_r.at[1], sibling)
    start([send_lo])

    @pl.loop(0, TOK // 16)
    def _(block):
        rows = pl.ds(pl.multiple_of(block * 16, 16), 16)
        h32 = hidden[rows, :].astype(F32)
        scale = lax.rsqrt(jnp.sum(h32 * h32, axis=1, keepdims=True) * (1.0 / 8192.0) + 1e-05)
        normed = (h32 * scale).astype(BF16)
        for owner in range(16):
            for quarter in range(4):
                src = owner * 512 + quarter * 128
                xn[quarter, rows, pl.ds(owner * 128, 128)] = normed[:, src:src + 128]

    send_x = [
        remote(xn.at[1 - odd], xz.at[0, c], x_s.at[0], x_r.at[0], partner),
        remote(xn.at[3 - odd], xz.at[1, c], x_s.at[1], x_r.at[1], sharer),
        remote(xn.at[odd], xo.at[0, c], x_s.at[2], x_r.at[2], sibling),
        remote(xn.at[2 + odd], xo.at[1, c], x_s.at[3], x_r.at[3], sibling),
    ]
    start(send_x)
    local_x = [pltpu.make_async_copy(xn.at[2 * i + odd], xo.at[i, c], loc.at[10 + i]) for i in range(2)]
    for copy in local_x:
        copy.start()

    def wo_first(s):
        local_wo[s].wait()
        start(wo[s][0])

    def wo_second_y(s):
        arrive(wo[s][0][:3])
        start(wo[s][1][:2])

    def wo_second_x(s):
        arrive(wo[s][0][3:])
        start(wo[s][1][2:])

    def wo_second(s):
        wo_second_x(s)
        wo_second_y(s)

    def wo_third(s):
        arrive(wo[s][1])
        start(wo[s][2])

    def wo_done(s):
        arrive(wo[s][2])

    arrive(kv1)
    start(kv2)
    wo_first(0)
    arrive(send_x[:2])
    pass_x = [remote(xz.at[i, c], xz.at[i, c], x_s.at[4 + i], x_r.at[4 + i], sibling) for i in range(2)]
    start(pass_x)
    arrive(kv2)
    start(kv3)
    wo_first(1)
    wo_first(2)
    arrive(send_x[2:])
    arrive(pass_x)
    for copy in local_x:
        copy.wait()
    arrive(kv3)

    def dot_kv(tokens, colour):
        return jnp.dot(
            tokens.reshape(2 * TOK, 2048), kvw[colour].reshape(2048, 512), preferred_element_type=F32
        ).reshape(2, TOK, 512)

    send_p = []
    for i, device in enumerate((partner, sharer)):
        part_z[i] = dot_kv(xz[i], i)
        send_p.append(remote(part_z.at[i], part_in.at[i], p_s.at[i], p_r.at[i], device))
        start(send_p[i:])
    part[...] = dot_kv(xo[0], 0)
    part[...] += dot_kv(xo[1], 1)

    wo_second(0)
    wo_first(3)
    wo_first(4)
    wo_third(0)
    arrive(send_p)
    total_kv = part[...] + part_in[0] + part_in[1]
    for j in range(2):
        for i in range(2):
            cols = slice(256 * i + HEAD * j, 256 * i + HEAD * (j + 1))
            win[j, :, 4, :, HEAD * i:HEAD * (i + 1)] = total_kv[:, :, cols].astype(BF16)
    send_win, pass_win, hops = [], [], (1, 3, 2)
    for j in range(2):
        send_win.append(remote(win.at[j, :, 4], win.at[j, :, 0], win_s.at[j, 0], win_r.at[j, 0], to_x[0]))
        pass_win.append([
            remote(
                win.at[j, :, jnp.where(y + d < 4, 4, 0)], win.at[j, :, 4 - d], win_s.at[j, d], win_r.at[j, d], to_y[k]
            )
            for k, d in enumerate(hops)
        ])

    def window_out(j):
        start(send_win[j:j + 1])
        for d, copy in zip(hops, pass_win[j]):
            pl.when(y + d < 4)(copy.start)
            flying.append(copy)

    def window_on(j):
        arrive(send_win[j:j + 1])
        for d, copy in zip(hops, pass_win[j]):
            pl.when(y + d >= 4)(copy.start)

    window_out(0)
    window_out(1)
    wo_second_x(1)
    wo_second_x(2)
    window_on(0)
    window_on(1)
    wo_second_y(1)
    wo_second_y(2)
    wo_done(0)
    start([share])
    wo_first(5)
    wo_first(6)
    local_q.wait()
    arrive([send_q])
    arrive([send_lo])
    arrive(pass_win[0])

    col = lax.broadcasted_iota(jnp.int32, (TOK, 5 * TOK), 1)
    row = lax.broadcasted_iota(jnp.int32, (TOK, 5 * TOK), 0)

    def attend(j):
        @pl.loop(0, 8)
        def _(step):
            r, pair = step // 4, lax.rem(step, 4)
            both = qb[r, :, pl.ds(pl.multiple_of(j * 1024 + pair * 256, 256), 256)]
            q = jnp.concatenate([both[:, :HEAD], both[:, HEAD:]], axis=0)
            k = win[j, r, :, :, pl.ds(0, HEAD)].reshape(5 * TOK, HEAD)
            v = win[j, r, :, :, pl.ds(HEAD, HEAD)].reshape(5 * TOK, HEAD)
            allowed = ((col.astype(F32) >= lo[r][:, :1]) & (col <= row + 4 * TOK))[None]
            s = lax.dot_general(q, k, (((1,), (1,)), ((), ())), preferred_element_type=F32)
            s = (s * (HEAD ** -0.5)).reshape(2, TOK, 5 * TOK)
            s = jnp.where(allowed, s, F32(-1e30))
            top = jnp.max(s, axis=2, keepdims=True)
            w = jnp.where(allowed, jnp.exp(s - top), F32(0.0))
            total = jnp.sum(w, axis=2, keepdims=True)
            mixed = jnp.dot(w.astype(BF16).reshape(2 * TOK, 5 * TOK), v, preferred_element_type=F32)
            mixed = (mixed.reshape(2, TOK, HEAD) / total).astype(BF16)
            at[2 * c + j, r, :, pl.ds(pl.multiple_of(pair * HEAD, HEAD), HEAD)] = mixed[0]
            at[2 * c + j, r, :, pl.ds(pl.multiple_of((4 + pair) * HEAD, HEAD), HEAD)] = mixed[1]

        mine = at.at[2 * c + j, pl.ds(0, 2)]
        theirs = at.at[2 * c + j, pl.ds(2, 2)]
        copies = [
            remote(mine, theirs, at_s.at[3 * j], at_r.at[3 * j], partner),
            remote(mine, mine, at_s.at[3 * j + 1], at_r.at[3 * j + 1], sibling),
            remote(theirs, theirs, at_s.at[3 * j + 2], at_r.at[3 * j + 2], sibling),
        ]
        start(copies[:2])
        return copies

    def pass_on(copies):
        arrive(copies[:1])
        start(copies[2:])

    heads0 = attend(0)
    wo_third(1)
    wo_second(3)
    arrive(pass_win[1])
    heads1 = attend(1)
    wo_third(2)
    wo_second(4)
    pass_on(heads0)
    wo_third(3)
    wo_second(5)
    pass_on(heads1)
    wo_third(4)
    wo_second(6)
    for copies in (heads0, heads1):
        arrive(copies[1:])

    outs = []

    def project(s):
        acc[...] = jnp.zeros_like(acc)

        @pl.loop(0, 4)
        def _(g):
            acc[...] += jnp.dot(
                at[g].reshape(4 * TOK, 1024), wb[s, g].reshape(1024, COLS), preferred_element_type=F32
            )

        ob[s] = acc[...].astype(BF16).reshape(4, TOK, COLS)
        cols = pl.ds(band_col(s), COLS)
        rb[:, cols] = ob[s, c]
        copies = [
            remote(ob.at[s, slot], rb.at[:, cols], ob_s.at[s, i], ob_r.at[s, i], device)
            for i, (slot, device) in enumerate(((2 + c, partner), (2 + other, cross), (other, sibling)))
        ]
        start(copies)
        outs.extend(copies)

    project(0)
    wo_done(1)
    project(1)
    wo_third(5)
    wo_done(2)
    project(2)
    wo_done(3)
    project(3)
    wo_third(6)
    wo_done(4)
    project(4)
    wo_done(5)
    project(5)
    arrive([share])
    project(7)
    wo_done(6)
    project(6)
    arrive(outs)
    write = pltpu.make_async_copy(rb, result, loc.at[12])
    write.start()

    finish()
    write.wait()


def body(hidden, queries, key_matrix, value_matrix, out_weight, lengths):
    dma = pltpu.SemaphoreType.DMA
    vmem, anywhere = pl.BlockSpec(memory_space=pltpu.VMEM), pl.BlockSpec(memory_space=pl.ANY)
    projected = pl.pallas_call(
        kernel,
        out_shape=jax.ShapeDtypeStruct((TOK, 8192), BF16),
        in_specs=[pl.BlockSpec(memory_space=pltpu.SMEM), vmem] + [anywhere] * 4,
        out_specs=anywhere,
        scratch_shapes=[
            pltpu.VMEM((4, TOK, 2048), BF16),
            pltpu.VMEM((2, 2, TOK, 2048), BF16),
            pltpu.VMEM((2, 2, TOK, 2048), BF16),
            pltpu.VMEM((2, 4, 4, 128, 512), BF16),
            pltpu.VMEM((2, TOK, 512), F32),
            pltpu.VMEM((2, 2, TOK, 512), F32),
            pltpu.VMEM((2, 2, TOK, 512), F32),
            pltpu.VMEM((2, 2, 5, TOK, 256), BF16),
            pltpu.VMEM((2, TOK, 2048), BF16),
            pltpu.VMEM((2, TOK, 128), F32),
            pltpu.VMEM((SLOTS, 4, 2, 4, 128, COLS), BF16),
            pltpu.VMEM((4, 4, TOK, 1024), BF16),
            pltpu.VMEM((SLOTS, 4, TOK, COLS), BF16),
            pltpu.VMEM((4 * TOK, COLS), F32),
            pltpu.VMEM((TOK, 8192), BF16),
            dma((14,)), dma((14,)),
            dma((SLOTS - 1, 14)), dma((SLOTS - 1, 14)),
            dma, dma,
            dma((6,)), dma((6,)),
            dma((2,)), dma((2,)),
            dma((2,)), dma((2,)),
            dma((2, 4)), dma((2, 4)),
            dma((6,)), dma((6,)),
            dma((SLOTS, 3)), dma((SLOTS, 3)),
            dma((13,)),
        ],
        compiler_params=pltpu.CompilerParams(
            collective_id=0, has_side_effects=True, vmem_limit_bytes=60 * 2 ** 20
        ),
        cost_estimate=pl.CostEstimate(flops=12 * 10 ** 9, bytes_accessed=16 * 2 ** 20, transcendentals=3 * 10 ** 6),
    )(
        lengths, hidden, queries,
        key_matrix.reshape(2, 2, 128, 512), value_matrix.reshape(2, 2, 128, 512), out_weight.reshape(2, 128, 8192),
    )
    return hidden.astype(F32) + projected.astype(F32)


def solution(mesh):
    placed = (
        P(("node", "fsdp"), None),
        P(("node", "fsdp"), None),
        P("fsdp", None),
        P("fsdp", None),
        P("fsdp", None),
        P("node", None),
    )
    return jax.shard_map(
        body, mesh=mesh, in_specs=placed, out_specs=P(("node", "fsdp"), None), check_vma=False
    )
```

```python
import jax
import jax.numpy as jnp
from jax import lax
from jax.experimental import pallas as pl
from jax.experimental.pallas import tpu as pltpu
from jax.sharding import PartitionSpec as P

MESH = pl.DeviceIdType.MESH
HEAD = 128
TOK = 128
SLOTS = 6
COLS = 256
F32 = jnp.float32
BF16 = jnp.bfloat16


def gather_copies(piece, ssem, rsem, place, peers):
    x, y = place
    to_x, to_y = peers

    def copy(index, ref, device):
        return pltpu.make_async_remote_copy(
            src_ref=ref, dst_ref=ref, send_sem=ssem.at[index], recv_sem=rsem.at[index],
            device_id=device, device_id_type=MESH,
        )

    xr, xl = lax.rem(x + 1, 4), lax.rem(x + 3, 4)
    yr, yl = lax.rem(y + 1, 4), lax.rem(y + 3, 4)
    every, low, high = slice(None), pl.ds(0, 2), pl.ds(2, 2)
    first = [copy(k, piece(x, 0, y), to_x[k]) for k in range(3)]
    first += [copy(3 + k, piece(x, 1, y), to_y[k]) for k in range(3)]
    second = [copy(6 + k, piece(every, 0, y), to_y[k]) for k in range(2)]
    second += [copy(8 + k, piece(x, 1, every), to_x[k]) for k in range(2)]
    third = [
        copy(10, piece(low, 0, yl), to_y[0]),
        copy(11, piece(high, 0, yr), to_y[1]),
        copy(12, piece(xl, 1, low), to_x[0]),
        copy(13, piece(xr, 1, high), to_x[1]),
    ]
    return first, second, third


def kernel(
    lengths, hidden, queries, key_w, value_w, out_w, result,
    xn, xo, xz, kvw, part, part_z, part_in, win, qb, lo, wb, at, ob, acc, rb,
    kv_s, kv_r, wo_s, wo_r, x_s, x_r, q_s, q_r, p_s, p_r,
    win_s, win_r, at_s, at_r, ob_s, ob_r, loc,
):
    node, f = lax.axis_index("node"), lax.axis_index("fsdp")
    z, c = node // 2, lax.rem(node, 2)
    x, y = f // 4, lax.rem(f, 4)
    odd = lax.rem(z, 2)
    other = 1 - c
    pz = z + 1 - 2 * odd
    sz = lax.rem(z + 7 + 2 * odd, 8)
    uz, dz = lax.rem(z + 1, 8), lax.rem(z + 7, 8)
    sibling = (z * 2 + other, f)
    partner = (pz * 2 + c, f)
    sharer = (sz * 2 + c, f)
    up, up_cross = (uz * 2 + c, f), (uz * 2 + other, f)
    down, down_cross = (dz * 2 + c, f), (dz * 2 + other, f)
    to_x = [(node, lax.rem(x + d, 4) * 4 + y) for d in (1, 3, 2)]
    to_y = [(node, x * 4 + lax.rem(y + d, 4)) for d in (1, 3, 2)]
    place, peers = (x, y), (to_x, to_y)

    def remote(src, dst, ssem, rsem, device):
        return pltpu.make_async_remote_copy(
            src_ref=src, dst_ref=dst, send_sem=ssem, recv_sem=rsem, device_id=device, device_id_type=MESH
        )

    flying, landed = [], set()

    def start(copies):
        for copy in copies:
            copy.start()
            flying.append(copy)

    def arrive(copies):
        for copy in copies:
            copy.wait_recv()
            landed.add(id(copy))

    def finish():
        for copy in flying:
            if id(copy) not in landed:
                copy.wait_recv()
        for copy in flying:
            copy.wait_send()

    def slot_col(s):
        group = lax.rem(z + 24 - 3 * (s // 2), 8)
        return pl.multiple_of(group * 1024 + c * 512 + (s % 2) * COLS, COLS)

    local_kv = [
        pltpu.make_async_copy(
            w.at[:, odd, :, pl.ds(pl.multiple_of(c * 256, 256), 256)],
            kvw.at[:, x, y, :, pl.ds(256 * i, 256)],
            loc.at[i],
        )
        for i, w in enumerate((key_w, value_w))
    ]
    for copy in local_kv:
        copy.start()
    local_wo = [
        pltpu.make_async_copy(out_w.at[:, :, pl.ds(slot_col(s), COLS)], wb.at[s, x, :, y], loc.at[2 + s])
        for s in range(SLOTS)
    ]
    for copy in local_wo:
        copy.start()
    local_q = pltpu.make_async_copy(
        queries.at[:, pl.ds(pl.multiple_of(c * 2048, 2048), 2048)], qb.at[c], loc.at[8]
    )
    local_q.start()

    barrier = pltpu.get_barrier_semaphore()
    greeted = [sibling, up, up_cross, down, down_cross] + to_x + to_y
    for device in greeted:
        pl.semaphore_signal(barrier, inc=1, device_id=device, device_id_type=MESH)
    pl.semaphore_wait(barrier, len(greeted))

    kv1, kv2, kv3 = gather_copies(lambda i, colour, k: kvw.at[colour, i, k], kv_s, kv_r, place, peers)
    wo = [
        gather_copies(lambda i, colour, k, s=s: wb.at[s, i, colour, k], wo_s.at[s], wo_r.at[s], place, peers)
        for s in range(SLOTS)
    ]

    for copy in local_kv:
        copy.wait()
    start(kv1)
    send_q = remote(
        queries.at[:, pl.ds(pl.multiple_of(other * 2048, 2048), 2048)], qb.at[c], q_s.at[0], q_r.at[0], sibling
    )
    start([send_q])

    pos = f * TOK + lax.broadcasted_iota(jnp.int32, (TOK, 128), 0)
    end = jnp.int32(0)
    first = jnp.zeros((TOK, 128), jnp.int32)
    for e in range(8):
        end = end + lengths[0, e]
        first = jnp.where(pos >= end, end, first)
    lo[c] = (first - f * TOK + 4 * TOK).astype(F32)
    send_lo = remote(lo.at[c], lo.at[c], q_s.at[1], q_r.at[1], sibling)
    start([send_lo])

    @pl.loop(0, TOK // 16)
    def _(block):
        rows = pl.ds(pl.multiple_of(block * 16, 16), 16)
        h32 = hidden[rows, :].astype(F32)
        scale = lax.rsqrt(jnp.sum(h32 * h32, axis=1, keepdims=True) * (1.0 / 8192.0) + 1e-05)
        normed = (h32 * scale).astype(BF16)
        for owner in range(16):
            for quarter in range(4):
                src = owner * 512 + quarter * 128
                xn[quarter, rows, pl.ds(owner * 128, 128)] = normed[:, src:src + 128]

    send_x = [
        remote(xn.at[1 - odd], xz.at[0, c], x_s.at[0], x_r.at[0], partner),
        remote(xn.at[3 - odd], xz.at[1, c], x_s.at[1], x_r.at[1], sharer),
        remote(xn.at[odd], xo.at[0, c], x_s.at[2], x_r.at[2], sibling),
        remote(xn.at[2 + odd], xo.at[1, c], x_s.at[3], x_r.at[3], sibling),
    ]
    start(send_x)
    local_x = [pltpu.make_async_copy(xn.at[2 * i + odd], xo.at[i, c], loc.at[10 + i]) for i in range(2)]
    for copy in local_x:
        copy.start()

    def wo_first(s):
        local_wo[s].wait()
        start(wo[s][0])

    def wo_second_y(s):
        arrive(wo[s][0][:3])
        start(wo[s][1][:2])

    def wo_second_x(s):
        arrive(wo[s][0][3:])
        start(wo[s][1][2:])

    def wo_second(s):
        wo_second_x(s)
        wo_second_y(s)

    def wo_third(s):
        arrive(wo[s][1])
        start(wo[s][2])

    def wo_done(s):
        arrive(wo[s][2])

    arrive(kv1)
    start(kv2)
    wo_first(0)
    arrive(send_x[:2])
    pass_x = [remote(xz.at[i, c], xz.at[i, c], x_s.at[4 + i], x_r.at[4 + i], sibling) for i in range(2)]
    start(pass_x)
    arrive(kv2)
    start(kv3)
    wo_first(1)
    wo_first(2)
    arrive(send_x[2:])
    arrive(pass_x)
    for copy in local_x:
        copy.wait()
    arrive(kv3)

    def dot_kv(tokens, colour):
        return jnp.dot(
            tokens.reshape(2 * TOK, 2048), kvw[colour].reshape(2048, 512), preferred_element_type=F32
        ).reshape(2, TOK, 512)

    send_p = []
    for i, device in enumerate((partner, sharer)):
        part_z[i] = dot_kv(xz[i], i)
        send_p.append(remote(part_z.at[i], part_in.at[i], p_s.at[i], p_r.at[i], device))
        start(send_p[i:])
    part[...] = dot_kv(xo[0], 0)
    part[...] += dot_kv(xo[1], 1)

    wo_second(0)
    wo_first(3)
    wo_first(4)
    wo_third(0)
    arrive(send_p)
    total_kv = part[...] + part_in[0] + part_in[1]
    for j in range(2):
        for i in range(2):
            cols = slice(256 * i + HEAD * j, 256 * i + HEAD * (j + 1))
            win[j, :, 4, :, HEAD * i:HEAD * (i + 1)] = total_kv[:, :, cols].astype(BF16)
    send_win, pass_win, hops = [], [], (1, 3, 2)
    for j in range(2):
        send_win.append(remote(win.at[j, :, 4], win.at[j, :, 0], win_s.at[j, 0], win_r.at[j, 0], to_x[0]))
        pass_win.append([
            remote(
                win.at[j, :, jnp.where(y + d < 4, 4, 0)], win.at[j, :, 4 - d], win_s.at[j, d], win_r.at[j, d], to_y[k]
            )
            for k, d in enumerate(hops)
        ])

    def window_out(j):
        start(send_win[j:j + 1])
        for d, copy in zip(hops, pass_win[j]):
            pl.when(y + d < 4)(copy.start)
            flying.append(copy)

    def window_on(j):
        arrive(send_win[j:j + 1])
        for d, copy in zip(hops, pass_win[j]):
            pl.when(y + d >= 4)(copy.start)

    window_out(0)
    window_out(1)
    wo_second_x(1)
    wo_second_x(2)
    window_on(0)
    window_on(1)
    wo_second_y(1)
    wo_second_y(2)
    wo_first(5)
    local_q.wait()
    arrive([send_q])
    arrive([send_lo])
    arrive(pass_win[0])

    col = lax.broadcasted_iota(jnp.int32, (TOK, 5 * TOK), 1)
    row = lax.broadcasted_iota(jnp.int32, (TOK, 5 * TOK), 0)

    def attend(j):
        @pl.loop(0, 8)
        def _(step):
            r, pair = step // 4, lax.rem(step, 4)
            both = qb[r, :, pl.ds(pl.multiple_of(j * 1024 + pair * 256, 256), 256)]
            q = jnp.concatenate([both[:, :HEAD], both[:, HEAD:]], axis=0)
            k = win[j, r, :, :, pl.ds(0, HEAD)].reshape(5 * TOK, HEAD)
            v = win[j, r, :, :, pl.ds(HEAD, HEAD)].reshape(5 * TOK, HEAD)
            allowed = ((col.astype(F32) >= lo[r][:, :1]) & (col <= row + 4 * TOK))[None]
            s = lax.dot_general(q, k, (((1,), (1,)), ((), ())), preferred_element_type=F32)
            s = (s * (HEAD ** -0.5)).reshape(2, TOK, 5 * TOK)
            s = jnp.where(allowed, s, F32(-1e30))
            top = jnp.max(s, axis=2, keepdims=True)
            w = jnp.where(allowed, jnp.exp(s - top), F32(0.0))
            total = jnp.sum(w, axis=2, keepdims=True)
            mixed = jnp.dot(w.astype(BF16).reshape(2 * TOK, 5 * TOK), v, preferred_element_type=F32)
            mixed = (mixed.reshape(2, TOK, HEAD) / total).astype(BF16)
            at[2 * c + j, 2 + r, :, pl.ds(pl.multiple_of(pair * HEAD, HEAD), HEAD)] = mixed[0]
            at[2 * c + j, 2 + r, :, pl.ds(pl.multiple_of((4 + pair) * HEAD, HEAD), HEAD)] = mixed[1]

        above, mine, below = (at.at[2 * c + j, pl.ds(2 * i, 2)] for i in range(3))
        copies = [
            remote(mine, below, at_s.at[j, 0], at_r.at[j, 0], up),
            remote(mine, above, at_s.at[j, 1], at_r.at[j, 1], down),
            remote(mine, mine, at_s.at[j, 2], at_r.at[j, 2], sibling),
            remote(below, below, at_s.at[j, 3], at_r.at[j, 3], sibling),
            remote(above, above, at_s.at[j, 4], at_r.at[j, 4], sibling),
        ]
        start(copies[:3])
        return copies

    def pass_on(copies):
        for i in range(2):
            arrive(copies[i:i + 1])
            start(copies[3 + i:4 + i])

    heads0 = attend(0)
    wo_third(1)
    wo_second(3)
    arrive(pass_win[1])
    heads1 = attend(1)
    wo_third(2)
    wo_second(4)
    pass_on(heads0)
    wo_third(3)
    wo_second(5)
    pass_on(heads1)
    for copies in (heads0, heads1):
        arrive(copies[2:])

    outs = []

    def project(s):
        low = 0 if s < 4 else 2
        rows = (6 - low) * TOK
        acc[:rows] = jnp.zeros((rows, COLS), F32)

        @pl.loop(0, 4)
        def _(g):
            acc[:rows] += jnp.dot(
                at[g, low:].reshape(rows, 1024), wb[s, g].reshape(1024, COLS), preferred_element_type=F32
            )

        ob[s, low:] = acc[:rows].astype(BF16).reshape(6 - low, TOK, COLS)
        cols = pl.ds(slot_col(s), COLS)
        rb[:, cols] = ob[s, 2 + c]
        targets = [(4 + c, down), (4 + other, down_cross), (c, up), (other, up_cross), (2 + other, sibling)]
        copies = [
            remote(ob.at[s, slot], rb.at[:, cols], ob_s.at[s, i], ob_r.at[s, i], device)
            for i, (slot, device) in enumerate(targets)
            if low == 0 or i not in (2, 3)
        ]
        start(copies)
        outs.extend(copies)

    wo_done(0)
    project(0)
    wo_third(4)
    wo_done(1)
    project(1)
    wo_done(2)
    project(2)
    wo_third(5)
    wo_done(3)
    project(3)
    wo_done(4)
    project(4)
    wo_done(5)
    project(5)
    arrive(outs)
    write = pltpu.make_async_copy(rb, result, loc.at[12])
    write.start()

    finish()
    write.wait()


def body(hidden, queries, key_matrix, value_matrix, out_weight, lengths):
    dma = pltpu.SemaphoreType.DMA
    vmem, anywhere = pl.BlockSpec(memory_space=pltpu.VMEM), pl.BlockSpec(memory_space=pl.ANY)
    projected = pl.pallas_call(
        kernel,
        out_shape=jax.ShapeDtypeStruct((TOK, 8192), BF16),
        in_specs=[pl.BlockSpec(memory_space=pltpu.SMEM), vmem] + [anywhere] * 4,
        out_specs=anywhere,
        scratch_shapes=[
            pltpu.VMEM((4, TOK, 2048), BF16),
            pltpu.VMEM((2, 2, TOK, 2048), BF16),
            pltpu.VMEM((2, 2, TOK, 2048), BF16),
            pltpu.VMEM((2, 4, 4, 128, 512), BF16),
            pltpu.VMEM((2, TOK, 512), F32),
            pltpu.VMEM((2, 2, TOK, 512), F32),
            pltpu.VMEM((2, 2, TOK, 512), F32),
            pltpu.VMEM((2, 2, 5, TOK, 256), BF16),
            pltpu.VMEM((2, TOK, 2048), BF16),
            pltpu.VMEM((2, TOK, 128), F32),
            pltpu.VMEM((SLOTS, 4, 2, 4, 128, COLS), BF16),
            pltpu.VMEM((4, 6, TOK, 1024), BF16),
            pltpu.VMEM((SLOTS, 6, TOK, COLS), BF16),
            pltpu.VMEM((6 * TOK, COLS), F32),
            pltpu.VMEM((TOK, 8192), BF16),
            dma((14,)), dma((14,)),
            dma((SLOTS, 14)), dma((SLOTS, 14)),
            dma((6,)), dma((6,)),
            dma((2,)), dma((2,)),
            dma((2,)), dma((2,)),
            dma((2, 4)), dma((2, 4)),
            dma((2, 5)), dma((2, 5)),
            dma((SLOTS, 5)), dma((SLOTS, 5)),
            dma((13,)),
        ],
        compiler_params=pltpu.CompilerParams(
            collective_id=0, has_side_effects=True, vmem_limit_bytes=60 * 2 ** 20
        ),
        cost_estimate=pl.CostEstimate(flops=12 * 10 ** 9, bytes_accessed=16 * 2 ** 20, transcendentals=3 * 10 ** 6),
    )(
        lengths, hidden, queries,
        key_matrix.reshape(2, 2, 128, 512), value_matrix.reshape(2, 2, 128, 512), out_weight.reshape(2, 128, 8192),
    )
    return hidden.astype(F32) + projected.astype(F32)


def solution(mesh):
    placed = (
        P(("node", "fsdp"), None),
        P(("node", "fsdp"), None),
        P("fsdp", None),
        P("fsdp", None),
        P("fsdp", None),
        P("node", None),
    )
    return jax.shard_map(
        body, mesh=mesh, in_specs=placed, out_specs=P(("node", "fsdp"), None), check_vma=False
    )
```

```python
import jax
import jax.numpy as jnp
from jax import lax
from jax.experimental import pallas as pl
from jax.experimental.pallas import tpu as pltpu
from jax.sharding import PartitionSpec as P

MESH = pl.DeviceIdType.MESH
HEAD = 128
TOK = 128
SLOTS = 6
COLS = 256
F32 = jnp.float32
BF16 = jnp.bfloat16


def gather_copies(piece, ssem, rsem, place, peers):
    x, y = place
    to_x, to_y = peers

    def copy(index, ref, device):
        return pltpu.make_async_remote_copy(
            src_ref=ref, dst_ref=ref, send_sem=ssem.at[index], recv_sem=rsem.at[index],
            device_id=device, device_id_type=MESH,
        )

    xr, xl = lax.rem(x + 1, 4), lax.rem(x + 3, 4)
    yr, yl = lax.rem(y + 1, 4), lax.rem(y + 3, 4)
    every, low, high = slice(None), pl.ds(0, 2), pl.ds(2, 2)
    first = [copy(k, piece(x, 0, y), to_x[k]) for k in range(3)]
    first += [copy(3 + k, piece(x, 1, y), to_y[k]) for k in range(3)]
    second = [copy(6 + k, piece(every, 0, y), to_y[k]) for k in range(2)]
    second += [copy(8 + k, piece(x, 1, every), to_x[k]) for k in range(2)]
    third = [
        copy(10, piece(low, 0, yl), to_y[0]),
        copy(11, piece(high, 0, yr), to_y[1]),
        copy(12, piece(xl, 1, low), to_x[0]),
        copy(13, piece(xr, 1, high), to_x[1]),
    ]
    relay = [
        copy(2, piece(xl, 0, y).at[pl.ds(0, 64)], to_x[0]),
        copy(14, piece(xr, 0, y).at[pl.ds(64, 64)], to_x[1]),
        copy(5, piece(x, 1, yl).at[pl.ds(0, 64)], to_y[0]),
        copy(15, piece(x, 1, yr).at[pl.ds(64, 64)], to_y[1]),
    ]
    return first, second, third, relay


def kernel(
    lengths, hidden, queries, key_w, value_w, out_w, result,
    xn, xo, xz, kvw, part, part_z, part_in, win, qb, lo, wb, at, ob, acc, rb,
    kv_s, kv_r, wo_s, wo_r, x_s, x_r, q_s, q_r, p_s, p_r,
    win_s, win_r, at_s, at_r, ob_s, ob_r, loc,
):
    node, f = lax.axis_index("node"), lax.axis_index("fsdp")
    z, c = node // 2, lax.rem(node, 2)
    x, y = f // 4, lax.rem(f, 4)
    odd = lax.rem(z, 2)
    other = 1 - c
    pz = z + 1 - 2 * odd
    sz = lax.rem(z + 7 + 2 * odd, 8)
    uz, dz = lax.rem(z + 1, 8), lax.rem(z + 7, 8)
    sibling = (z * 2 + other, f)
    partner = (pz * 2 + c, f)
    sharer = (sz * 2 + c, f)
    up, up_cross = (uz * 2 + c, f), (uz * 2 + other, f)
    down, down_cross = (dz * 2 + c, f), (dz * 2 + other, f)
    to_x = [(node, lax.rem(x + d, 4) * 4 + y) for d in (1, 3, 2)]
    to_y = [(node, x * 4 + lax.rem(y + d, 4)) for d in (1, 3, 2)]
    place, peers = (x, y), (to_x, to_y)

    def remote(src, dst, ssem, rsem, device):
        return pltpu.make_async_remote_copy(
            src_ref=src, dst_ref=dst, send_sem=ssem, recv_sem=rsem, device_id=device, device_id_type=MESH
        )

    flying, landed = [], set()

    def start(copies):
        for copy in copies:
            copy.start()
            flying.append(copy)

    def arrive(copies):
        for copy in copies:
            copy.wait_recv()
            landed.add(id(copy))

    def finish():
        for copy in flying:
            if id(copy) not in landed:
                copy.wait_recv()
        for copy in flying:
            copy.wait_send()

    def slot_col(s):
        group = lax.rem(z + 24 - 3 * (s // 2), 8)
        return pl.multiple_of(group * 1024 + c * 512 + (s % 2) * COLS, COLS)

    local_kv = [
        pltpu.make_async_copy(
            w.at[:, odd, :, pl.ds(pl.multiple_of((2 * c + j) * HEAD, HEAD), HEAD)],
            kvw.at[:, x, y, :, pl.ds((2 * j + i) * HEAD, HEAD)],
            loc.at[11 + 2 * j + i],
        )
        for i, w in enumerate((key_w, value_w))
        for j in range(2)
    ]
    for copy in local_kv:
        copy.start()
    local_wo = [
        pltpu.make_async_copy(out_w.at[:, :, pl.ds(slot_col(s), COLS)], wb.at[s, x, :, y], loc.at[s])
        for s in range(SLOTS)
    ]
    for copy in local_wo:
        copy.start()
    local_q = pltpu.make_async_copy(
        queries.at[:, pl.ds(pl.multiple_of(c * 2048, 2048), 2048)], qb.at[c], loc.at[6]
    )
    local_q.start()

    barrier = pltpu.get_barrier_semaphore()
    greeted = [sibling, up, up_cross, down, down_cross] + to_x + to_y
    for device in greeted:
        pl.semaphore_signal(barrier, inc=1, device_id=device, device_id_type=MESH)
    pl.semaphore_wait(barrier, len(greeted))

    kv1, kv2, kv3, _ = gather_copies(lambda i, colour, k: kvw.at[colour, i, k], kv_s, kv_r, place, peers)
    wo = [
        gather_copies(lambda i, colour, k, s=s: wb.at[s, i, colour, k], wo_s.at[s], wo_r.at[s], place, peers)
        for s in range(SLOTS)
    ]

    for copy in local_kv:
        copy.wait()
    start(kv1)
    send_q = remote(
        queries.at[:, pl.ds(pl.multiple_of(other * 2048, 2048), 2048)], qb.at[c], q_s.at[0], q_r.at[0], sibling
    )
    start([send_q])

    pos = f * TOK + lax.broadcasted_iota(jnp.int32, (TOK, 128), 0)
    end = jnp.int32(0)
    first = jnp.zeros((TOK, 128), jnp.int32)
    for e in range(8):
        end = end + lengths[0, e]
        first = jnp.where(pos >= end, end, first)
    lo[c] = (first - f * TOK + 4 * TOK).astype(F32)
    send_lo = remote(lo.at[c], lo.at[c], q_s.at[1], q_r.at[1], sibling)
    start([send_lo])

    @pl.loop(0, TOK // 16)
    def _(block):
        rows = pl.ds(pl.multiple_of(block * 16, 16), 16)
        h32 = hidden[rows, :].astype(F32)
        scale = lax.rsqrt(jnp.sum(h32 * h32, axis=1, keepdims=True) * (1.0 / 8192.0) + 1e-05)
        normed = (h32 * scale).astype(BF16)
        for owner in range(16):
            for quarter in range(4):
                src = owner * 512 + quarter * 128
                xn[quarter, rows, pl.ds(owner * 128, 128)] = normed[:, src:src + 128]

    send_x = [
        remote(xn.at[1 - odd], xz.at[0, c], x_s.at[0], x_r.at[0], partner),
        remote(xn.at[3 - odd], xz.at[1, c], x_s.at[1], x_r.at[1], sharer),
        remote(xn.at[odd], xo.at[0, c], x_s.at[2], x_r.at[2], sibling),
        remote(xn.at[2 + odd], xo.at[1, c], x_s.at[3], x_r.at[3], sibling),
    ]
    start(send_x)
    local_x = [pltpu.make_async_copy(xn.at[2 * i + odd], xo.at[i, c], loc.at[7 + i]) for i in range(2)]
    for copy in local_x:
        copy.start()

    def wo_first(s):
        local_wo[s].wait()
        start(wo[s][0][:2] + wo[s][0][3:5])

    def wo_relay(s):
        arrive(wo[s][0][:2] + wo[s][0][3:5])
        start(wo[s][3])

    def wo_second_y(s):
        arrive(wo[s][3][:2])
        start(wo[s][1][:2])

    def wo_second_x(s):
        arrive(wo[s][3][2:])
        start(wo[s][1][2:])

    def wo_second(s):
        wo_second_x(s)
        wo_second_y(s)

    def wo_third(s):
        arrive(wo[s][1])
        start(wo[s][2])

    def wo_done(s):
        arrive(wo[s][2])

    arrive(kv1)
    start(kv2)
    wo_first(0)
    arrive(send_x[:2])
    pass_x = [remote(xz.at[i, c], xz.at[i, c], x_s.at[4 + i], x_r.at[4 + i], sibling) for i in range(2)]
    start(pass_x)
    arrive(kv2)
    start(kv3)
    wo_relay(0)
    wo_first(1)
    wo_first(2)
    arrive(send_x[2:])
    arrive(pass_x)
    for copy in local_x:
        copy.wait()
    arrive(kv3)

    def dot_kv(tokens, colour):
        return jnp.dot(
            tokens.reshape(2 * TOK, 2048), kvw[colour].reshape(2048, 512), preferred_element_type=F32
        ).reshape(2, TOK, 512)

    send_p = [[], []]
    for i, device in enumerate((partner, sharer)):
        both = dot_kv(xz[i], i)
        for j in range(2):
            part_z[i, j] = both[:, :, 256 * j:256 * (j + 1)]
            send_p[j].append(remote(part_z.at[i, j], part_in.at[i, j], p_s.at[i, j], p_r.at[i, j], device))
            start(send_p[j][i:])
    part[...] = dot_kv(xo[0], 0)
    part[...] += dot_kv(xo[1], 1)

    wo_relay(1)
    wo_second(0)
    wo_relay(2)
    wo_first(3)

    send_win, pass_win, hops = [], [], (1, 3, 2)
    for j in range(2):
        send_win.append(remote(win.at[j, :, 4], win.at[j, :, 0], win_s.at[j, 0], win_r.at[j, 0], to_x[0]))
        pass_win.append([
            remote(
                win.at[j, :, jnp.where(y + d < 4, 4, 0)], win.at[j, :, 4 - d], win_s.at[j, d], win_r.at[j, d], to_y[k]
            )
            for k, d in enumerate(hops)
        ])

    def window_out(j):
        arrive(send_p[j])
        own = part[:, :, 256 * j:256 * (j + 1)] + part_in[0, j] + part_in[1, j]
        win[j, :, 4] = own.astype(BF16)
        start(send_win[j:j + 1])
        for d, copy in zip(hops, pass_win[j]):
            pl.when(y + d < 4)(copy.start)
            flying.append(copy)

    def window_on(j):
        arrive(send_win[j:j + 1])
        for d, copy in zip(hops, pass_win[j]):
            pl.when(y + d >= 4)(copy.start)

    window_out(0)
    window_out(1)
    wo_second_x(1)
    wo_second_x(2)
    window_on(0)
    window_on(1)
    wo_third(0)
    wo_relay(3)
    wo_first(4)
    wo_second_y(1)
    wo_second_y(2)
    wo_relay(4)
    wo_first(5)
    local_q.wait()
    arrive([send_q])
    arrive([send_lo])
    arrive(pass_win[0])

    col = lax.broadcasted_iota(jnp.int32, (TOK, 5 * TOK), 1)
    row = lax.broadcasted_iota(jnp.int32, (TOK, 5 * TOK), 0)

    def attend(j):
        @pl.loop(0, 8)
        def _(step):
            r, pair = step // 4, lax.rem(step, 4)
            both = qb[r, :, pl.ds(pl.multiple_of(j * 1024 + pair * 256, 256), 256)]
            q = jnp.concatenate([both[:, :HEAD], both[:, HEAD:]], axis=0)
            k = win[j, r, :, :, pl.ds(0, HEAD)].reshape(5 * TOK, HEAD)
            v = win[j, r, :, :, pl.ds(HEAD, HEAD)].reshape(5 * TOK, HEAD)
            allowed = ((col.astype(F32) >= lo[r][:, :1]) & (col <= row + 4 * TOK))[None]
            s = lax.dot_general(q, k, (((1,), (1,)), ((), ())), preferred_element_type=F32)
            s = (s * (HEAD ** -0.5)).reshape(2, TOK, 5 * TOK)
            s = jnp.where(allowed, s, F32(-1e30))
            top = jnp.max(s, axis=2, keepdims=True)
            w = jnp.where(allowed, jnp.exp(s - top), F32(0.0))
            total = jnp.sum(w, axis=2, keepdims=True)
            mixed = jnp.dot(w.astype(BF16).reshape(2 * TOK, 5 * TOK), v, preferred_element_type=F32)
            mixed = (mixed.reshape(2, TOK, HEAD) / total).astype(BF16)
            at[2 * c + j, 2 + r, :, pl.ds(pl.multiple_of(pair * HEAD, HEAD), HEAD)] = mixed[0]
            at[2 * c + j, 2 + r, :, pl.ds(pl.multiple_of((4 + pair) * HEAD, HEAD), HEAD)] = mixed[1]

        above, mine, below = (at.at[2 * c + j, pl.ds(2 * i, 2)] for i in range(3))
        copies = [
            remote(mine, below, at_s.at[j, 0], at_r.at[j, 0], up),
            remote(mine, above, at_s.at[j, 1], at_r.at[j, 1], down),
            remote(mine, mine, at_s.at[j, 2], at_r.at[j, 2], sibling),
            remote(below, below, at_s.at[j, 3], at_r.at[j, 3], sibling),
            remote(above, above, at_s.at[j, 4], at_r.at[j, 4], sibling),
        ]
        start(copies[:3])
        return copies

    def pass_on(copies):
        for i in range(2):
            arrive(copies[i:i + 1])
            start(copies[3 + i:4 + i])

    heads0 = attend(0)
    wo_relay(5)
    wo_second(3)
    wo_second(4)
    wo_third(1)
    arrive(pass_win[1])
    heads1 = attend(1)
    wo_second(5)
    pass_on(heads0)
    wo_third(2)
    pass_on(heads1)
    wo_third(3)
    for copies in (heads0, heads1):
        arrive(copies[2:])

    outs = []

    def project(s):
        low, high = (2 if s >= 4 else 0), 6
        rows = (high - low) * TOK
        acc[:rows] = jnp.zeros((rows, COLS), F32)

        @pl.loop(0, 4)
        def _(g):
            acc[:rows] += jnp.dot(
                at[g, low:high].reshape(rows, 1024), wb[s, g].reshape(1024, COLS), preferred_element_type=F32
            )

        ob[s, low:high] = acc[:rows].astype(BF16).reshape(high - low, TOK, COLS)
        cols = pl.ds(slot_col(s), COLS)
        rb[:, cols] = ob[s, 2 + c]
        targets = [(4 + c, down), (4 + other, down_cross), (c, up), (other, up_cross), (2 + other, sibling)]
        slot_low = (4, 4, 0, 0, 2)
        copies = [
            remote(ob.at[s, slot], rb.at[:, cols], ob_s.at[s, i], ob_r.at[s, i], device)
            for i, (slot, device) in enumerate(targets)
            if low <= slot_low[i] < high
        ]
        start(copies)
        outs.extend(copies)

    wo_done(0)
    project(0)
    wo_done(1)
    project(1)
    wo_third(4)
    wo_done(2)
    project(2)
    wo_third(5)
    wo_done(3)
    project(3)
    wo_done(4)
    project(4)
    wo_done(5)
    project(5)
    arrive(outs)
    write = pltpu.make_async_copy(rb, result, loc.at[9])
    write.start()

    finish()
    write.wait()


def body(hidden, queries, key_matrix, value_matrix, out_weight, lengths):
    dma = pltpu.SemaphoreType.DMA
    vmem, anywhere = pl.BlockSpec(memory_space=pltpu.VMEM), pl.BlockSpec(memory_space=pl.ANY)
    projected = pl.pallas_call(
        kernel,
        out_shape=jax.ShapeDtypeStruct((TOK, 8192), BF16),
        in_specs=[pl.BlockSpec(memory_space=pltpu.SMEM), vmem] + [anywhere] * 4,
        out_specs=anywhere,
        scratch_shapes=[
            pltpu.VMEM((4, TOK, 2048), BF16),
            pltpu.VMEM((2, 2, TOK, 2048), BF16),
            pltpu.VMEM((2, 2, TOK, 2048), BF16),
            pltpu.VMEM((2, 4, 4, 128, 512), BF16),
            pltpu.VMEM((2, TOK, 512), F32),
            pltpu.VMEM((2, 2, 2, TOK, 256), F32),
            pltpu.VMEM((2, 2, 2, TOK, 256), F32),
            pltpu.VMEM((2, 2, 5, TOK, 256), BF16),
            pltpu.VMEM((2, TOK, 2048), BF16),
            pltpu.VMEM((2, TOK, 128), F32),
            pltpu.VMEM((SLOTS, 4, 2, 4, 128, COLS), BF16),
            pltpu.VMEM((4, 6, TOK, 1024), BF16),
            pltpu.VMEM((SLOTS, 6, TOK, COLS), BF16),
            pltpu.VMEM((6 * TOK, COLS), F32),
            pltpu.VMEM((TOK, 8192), BF16),
            dma((16,)), dma((16,)),
            dma((SLOTS, 16)), dma((SLOTS, 16)),
            dma((6,)), dma((6,)),
            dma((2,)), dma((2,)),
            dma((2, 2)), dma((2, 2)),
            dma((2, 4)), dma((2, 4)),
            dma((2, 5)), dma((2, 5)),
            dma((SLOTS, 5)), dma((SLOTS, 5)),
            dma((15,)),
        ],
        compiler_params=pltpu.CompilerParams(
            collective_id=0, has_side_effects=True, vmem_limit_bytes=60 * 2 ** 20
        ),
        cost_estimate=pl.CostEstimate(flops=12 * 10 ** 9, bytes_accessed=16 * 2 ** 20, transcendentals=3 * 10 ** 6),
    )(
        lengths, hidden, queries,
        key_matrix.reshape(2, 2, 128, 512), value_matrix.reshape(2, 2, 128, 512), out_weight.reshape(2, 128, 8192),
    )
    return hidden.astype(F32) + projected.astype(F32)


def solution(mesh):
    placed = (
        P(("node", "fsdp"), None),
        P(("node", "fsdp"), None),
        P("fsdp", None),
        P("fsdp", None),
        P("fsdp", None),
        P("node", None),
    )
    return jax.shard_map(
        body, mesh=mesh, in_specs=placed, out_specs=P(("node", "fsdp"), None), check_vma=False
    )
```

```python
import jax
import jax.numpy as jnp
from jax import lax
from jax.experimental import pallas as pl
from jax.experimental.pallas import tpu as pltpu
from jax.sharding import PartitionSpec as P

MESH = pl.DeviceIdType.MESH
HEAD = 128
TOK = 128
SLOTS = 6
COLS = 256
F32 = jnp.float32
BF16 = jnp.bfloat16


def gather_copies(piece, ssem, rsem, place, peers):
    x, y = place
    to_x, to_y = peers

    def copy(index, ref, device):
        return pltpu.make_async_remote_copy(
            src_ref=ref, dst_ref=ref, send_sem=ssem.at[index], recv_sem=rsem.at[index],
            device_id=device, device_id_type=MESH,
        )

    xr, xl = lax.rem(x + 1, 4), lax.rem(x + 3, 4)
    yr, yl = lax.rem(y + 1, 4), lax.rem(y + 3, 4)
    every, low, high = slice(None), pl.ds(0, 2), pl.ds(2, 2)
    first = [copy(k, piece(x, 0, y), to_x[k]) for k in range(3)]
    first += [copy(3 + k, piece(x, 1, y), to_y[k]) for k in range(3)]
    second = [copy(6 + k, piece(every, 0, y), to_y[k]) for k in range(2)]
    second += [copy(8 + k, piece(x, 1, every), to_x[k]) for k in range(2)]
    third = [
        copy(10, piece(low, 0, yl), to_y[0]),
        copy(11, piece(high, 0, yr), to_y[1]),
        copy(12, piece(xl, 1, low), to_x[0]),
        copy(13, piece(xr, 1, high), to_x[1]),
    ]
    relay = [
        copy(2, piece(xl, 0, y).at[pl.ds(0, 64)], to_x[0]),
        copy(14, piece(xr, 0, y).at[pl.ds(64, 64)], to_x[1]),
        copy(5, piece(x, 1, yl).at[pl.ds(0, 64)], to_y[0]),
        copy(15, piece(x, 1, yr).at[pl.ds(64, 64)], to_y[1]),
    ]
    return first, second, third, relay


def kernel(
    lengths, hidden, queries, key_w, value_w, out_w, result,
    xn, xo, xz, kvw, part, part_z, part_in, win, qb, lo, wb, at, ob, acc, rb,
    kv_s, kv_r, wo_s, wo_r, x_s, x_r, q_s, q_r, p_s, p_r,
    win_s, win_r, at_s, at_r, ob_s, ob_r, loc,
):
    node, f = lax.axis_index("node"), lax.axis_index("fsdp")
    z, c = node // 2, lax.rem(node, 2)
    x, y = f // 4, lax.rem(f, 4)
    odd = lax.rem(z, 2)
    other = 1 - c
    pz = z + 1 - 2 * odd
    sz = lax.rem(z + 7 + 2 * odd, 8)
    uz, dz = lax.rem(z + 1, 8), lax.rem(z + 7, 8)
    sibling = (z * 2 + other, f)
    partner = (pz * 2 + c, f)
    sharer = (sz * 2 + c, f)
    up, up_cross = (uz * 2 + c, f), (uz * 2 + other, f)
    down, down_cross = (dz * 2 + c, f), (dz * 2 + other, f)
    to_x = [(node, lax.rem(x + d, 4) * 4 + y) for d in (1, 3, 2)]
    to_y = [(node, x * 4 + lax.rem(y + d, 4)) for d in (1, 3, 2)]
    place, peers = (x, y), (to_x, to_y)

    def remote(src, dst, ssem, rsem, device):
        return pltpu.make_async_remote_copy(
            src_ref=src, dst_ref=dst, send_sem=ssem, recv_sem=rsem, device_id=device, device_id_type=MESH
        )

    flying, landed = [], set()

    def start(copies):
        for copy in copies:
            copy.start()
            flying.append(copy)

    def arrive(copies):
        for copy in copies:
            copy.wait_recv()
            landed.add(id(copy))

    def finish():
        for copy in flying:
            if id(copy) not in landed:
                copy.wait_recv()
        for copy in flying:
            copy.wait_send()

    def slot_col(s):
        group = lax.rem(z + 24 - 3 * (s // 2), 8)
        return pl.multiple_of(group * 1024 + c * 512 + (s % 2) * COLS, COLS)

    local_kv = [
        pltpu.make_async_copy(
            w.at[:, odd, :, pl.ds(pl.multiple_of((2 * c + j) * HEAD, HEAD), HEAD)],
            kvw.at[:, x, y, :, pl.ds((2 * j + i) * HEAD, HEAD)],
            loc.at[11 + 2 * j + i],
        )
        for i, w in enumerate((key_w, value_w))
        for j in range(2)
    ]
    for copy in local_kv:
        copy.start()
    local_wo = [
        pltpu.make_async_copy(out_w.at[:, :, pl.ds(slot_col(s), COLS)], wb.at[s, x, :, y], loc.at[s])
        for s in range(SLOTS)
    ]
    for copy in local_wo:
        copy.start()
    local_q = pltpu.make_async_copy(
        queries.at[:, pl.ds(pl.multiple_of(c * 2048, 2048), 2048)], qb.at[c], loc.at[6]
    )
    local_q.start()

    barrier = pltpu.get_barrier_semaphore()
    greeted = [sibling, up, up_cross, down, down_cross] + to_x + to_y
    for device in greeted:
        pl.semaphore_signal(barrier, inc=1, device_id=device, device_id_type=MESH)
    pl.semaphore_wait(barrier, len(greeted))

    kv1, kv2, kv3, _ = gather_copies(lambda i, colour, k: kvw.at[colour, i, k], kv_s, kv_r, place, peers)
    wo = [
        gather_copies(lambda i, colour, k, s=s: wb.at[s, i, colour, k], wo_s.at[s], wo_r.at[s], place, peers)
        for s in range(SLOTS)
    ]

    for copy in local_kv:
        copy.wait()
    start(kv1)
    send_q = remote(
        queries.at[:, pl.ds(pl.multiple_of(other * 2048, 2048), 2048)], qb.at[c], q_s.at[0], q_r.at[0], sibling
    )
    start([send_q])

    pos = f * TOK + lax.broadcasted_iota(jnp.int32, (TOK, 128), 0)
    end = jnp.int32(0)
    first = jnp.zeros((TOK, 128), jnp.int32)
    for e in range(8):
        end = end + lengths[0, e]
        first = jnp.where(pos >= end, end, first)
    lo[c] = (first - f * TOK + 4 * TOK).astype(F32)
    send_lo = remote(lo.at[c], lo.at[c], q_s.at[1], q_r.at[1], sibling)
    start([send_lo])

    @pl.loop(0, TOK // 16)
    def _(block):
        rows = pl.ds(pl.multiple_of(block * 16, 16), 16)
        h32 = hidden[rows, :].astype(F32)
        scale = lax.rsqrt(jnp.sum(h32 * h32, axis=1, keepdims=True) * (1.0 / 8192.0) + 1e-05)
        normed = (h32 * scale).astype(BF16)
        for owner in range(16):
            for quarter in range(4):
                src = owner * 512 + quarter * 128
                xn[quarter, rows, pl.ds(owner * 128, 128)] = normed[:, src:src + 128]

    send_x = [
        remote(xn.at[1 - odd], xz.at[0, c], x_s.at[0], x_r.at[0], partner),
        remote(xn.at[3 - odd], xz.at[1, c], x_s.at[1], x_r.at[1], sharer),
        remote(xn.at[odd], xo.at[0, c], x_s.at[2], x_r.at[2], sibling),
        remote(xn.at[2 + odd], xo.at[1, c], x_s.at[3], x_r.at[3], sibling),
    ]
    start(send_x)
    local_x = [pltpu.make_async_copy(xn.at[2 * i + odd], xo.at[i, c], loc.at[7 + i]) for i in range(2)]
    for copy in local_x:
        copy.start()

    def wo_first(s):
        local_wo[s].wait()
        start(wo[s][0][:2] + wo[s][0][3:5])

    def wo_relay(s):
        arrive(wo[s][0][:2] + wo[s][0][3:5])
        start(wo[s][3])

    def wo_second_y(s):
        arrive(wo[s][3][:2])
        start(wo[s][1][:2])

    def wo_second_x(s):
        arrive(wo[s][3][2:])
        start(wo[s][1][2:])

    def wo_second(s):
        wo_second_x(s)
        wo_second_y(s)

    def wo_third(s):
        arrive(wo[s][1])
        start(wo[s][2])

    def wo_done(s):
        arrive(wo[s][2])

    arrive(kv1)
    start(kv2)
    wo_first(0)
    arrive(send_x[:2])
    pass_x = [remote(xz.at[i, c], xz.at[i, c], x_s.at[4 + i], x_r.at[4 + i], sibling) for i in range(2)]
    start(pass_x)
    arrive(kv2)
    start(kv3)
    wo_relay(0)
    wo_first(1)
    wo_first(2)
    arrive(send_x[2:])
    arrive(pass_x)
    for copy in local_x:
        copy.wait()
    arrive(kv3)

    def dot_kv(tokens, colour):
        return jnp.dot(
            tokens.reshape(2 * TOK, 2048), kvw[colour].reshape(2048, 512), preferred_element_type=F32
        ).reshape(2, TOK, 512)

    send_p = [[], []]
    for i, device in enumerate((partner, sharer)):
        both = dot_kv(xz[i], i)
        for j in range(2):
            part_z[i, j] = both[:, :, 256 * j:256 * (j + 1)]
            send_p[j].append(remote(part_z.at[i, j], part_in.at[i, j], p_s.at[i, j], p_r.at[i, j], device))
            start(send_p[j][i:])
    part[...] = dot_kv(xo[0], 0)
    part[...] += dot_kv(xo[1], 1)

    wo_relay(1)
    wo_second(0)
    wo_relay(2)
    wo_first(3)

    send_win, pass_win, hops = [], [], (1, 3, 2)
    for j in range(2):
        send_win.append(remote(win.at[j, :, 4], win.at[j, :, 0], win_s.at[j, 0], win_r.at[j, 0], to_x[0]))
        pass_win.append([
            remote(
                win.at[j, :, jnp.where(y + d < 4, 4, 0)], win.at[j, :, 4 - d], win_s.at[j, d], win_r.at[j, d], to_y[k]
            )
            for k, d in enumerate(hops)
        ])

    def window_out(j):
        arrive(send_p[j])
        own = part[:, :, 256 * j:256 * (j + 1)] + part_in[0, j] + part_in[1, j]
        win[j, :, 4] = own.astype(BF16)
        start(send_win[j:j + 1])
        for d, copy in zip(hops, pass_win[j]):
            pl.when(y + d < 4)(copy.start)
            flying.append(copy)

    def window_on(j):
        arrive(send_win[j:j + 1])
        for d, copy in zip(hops, pass_win[j]):
            pl.when(y + d >= 4)(copy.start)

    window_out(0)
    window_out(1)
    wo_second_x(1)
    wo_second_x(2)
    window_on(0)
    window_on(1)
    wo_third(0)
    wo_relay(3)
    wo_first(4)
    wo_second_y(1)
    wo_second_y(2)
    wo_relay(4)
    wo_first(5)
    local_q.wait()
    arrive([send_q])
    arrive([send_lo])
    arrive(pass_win[0])

    col = lax.broadcasted_iota(jnp.int32, (TOK, 5 * TOK), 1)
    row = lax.broadcasted_iota(jnp.int32, (TOK, 5 * TOK), 0)

    def attend(j):
        @pl.loop(0, 8)
        def _(step):
            r, pair = step // 4, lax.rem(step, 4)
            both = qb[r, :, pl.ds(pl.multiple_of(j * 1024 + pair * 256, 256), 256)]
            q = jnp.concatenate([both[:, :HEAD], both[:, HEAD:]], axis=0)
            k = win[j, r, :, :, pl.ds(0, HEAD)].reshape(5 * TOK, HEAD)
            v = win[j, r, :, :, pl.ds(HEAD, HEAD)].reshape(5 * TOK, HEAD)
            allowed = ((col.astype(F32) >= lo[r][:, :1]) & (col <= row + 4 * TOK))[None]
            s = lax.dot_general(q, k, (((1,), (1,)), ((), ())), preferred_element_type=F32)
            s = (s * (HEAD ** -0.5)).reshape(2, TOK, 5 * TOK)
            s = jnp.where(allowed, s, F32(-1e30))
            top = jnp.max(s, axis=2, keepdims=True)
            w = jnp.where(allowed, jnp.exp(s - top), F32(0.0))
            total = jnp.sum(w, axis=2, keepdims=True)
            mixed = jnp.dot(w.astype(BF16).reshape(2 * TOK, 5 * TOK), v, preferred_element_type=F32)
            mixed = (mixed.reshape(2, TOK, HEAD) / total).astype(BF16)
            at[2 * c + j, 2 + r, :, pl.ds(pl.multiple_of(pair * HEAD, HEAD), HEAD)] = mixed[0]
            at[2 * c + j, 2 + r, :, pl.ds(pl.multiple_of((4 + pair) * HEAD, HEAD), HEAD)] = mixed[1]

        above, mine, below = (at.at[2 * c + j, pl.ds(2 * i, 2)] for i in range(3))
        copies = [
            remote(mine, below, at_s.at[j, 0], at_r.at[j, 0], up),
            remote(mine, above, at_s.at[j, 1], at_r.at[j, 1], down),
            remote(mine, mine, at_s.at[j, 2], at_r.at[j, 2], sibling),
            remote(below, below, at_s.at[j, 3], at_r.at[j, 3], sibling),
            remote(above, above, at_s.at[j, 4], at_r.at[j, 4], sibling),
        ]
        start(copies[:3])
        return copies

    def pass_on(copies):
        for i in range(2):
            arrive(copies[i:i + 1])
            start(copies[3 + i:4 + i])

    heads0 = attend(0)
    wo_relay(5)
    wo_second(3)
    wo_second(4)
    wo_third(1)
    arrive(pass_win[1])
    heads1 = attend(1)
    wo_second(5)
    pass_on(heads0)
    pass_on(heads1)
    wo_third(2)
    wo_third(3)
    for copies in (heads0, heads1):
        arrive(copies[2:])

    outs = []

    def project(s):
        low, high = (2 if s >= 4 else 0), 6
        rows = (high - low) * TOK
        acc[:rows] = jnp.zeros((rows, COLS), F32)

        @pl.loop(0, 4)
        def _(g):
            acc[:rows] += jnp.dot(
                at[g, low:high].reshape(rows, 1024), wb[s, g].reshape(1024, COLS), preferred_element_type=F32
            )

        ob[s, low:high] = acc[:rows].astype(BF16).reshape(high - low, TOK, COLS)
        cols = pl.ds(slot_col(s), COLS)
        rb[:, cols] = ob[s, 2 + c]
        targets = [(4 + c, down), (4 + other, down_cross), (c, up), (other, up_cross), (2 + other, sibling)]
        slot_low = (4, 4, 0, 0, 2)
        copies = [
            remote(ob.at[s, slot], rb.at[:, cols], ob_s.at[s, i], ob_r.at[s, i], device)
            for i, (slot, device) in enumerate(targets)
            if low <= slot_low[i] < high
        ]
        start(copies)
        outs.extend(copies)

    wo_done(0)
    project(0)
    wo_done(1)
    project(1)
    wo_third(4)
    wo_done(2)
    project(2)
    wo_third(5)
    wo_done(3)
    project(3)
    wo_done(4)
    project(4)
    wo_done(5)
    project(5)
    arrive(outs)
    write = pltpu.make_async_copy(rb, result, loc.at[9])
    write.start()

    finish()
    write.wait()


def body(hidden, queries, key_matrix, value_matrix, out_weight, lengths):
    dma = pltpu.SemaphoreType.DMA
    vmem, anywhere = pl.BlockSpec(memory_space=pltpu.VMEM), pl.BlockSpec(memory_space=pl.ANY)
    projected = pl.pallas_call(
        kernel,
        out_shape=jax.ShapeDtypeStruct((TOK, 8192), BF16),
        in_specs=[pl.BlockSpec(memory_space=pltpu.SMEM), vmem] + [anywhere] * 4,
        out_specs=anywhere,
        scratch_shapes=[
            pltpu.VMEM((4, TOK, 2048), BF16),
            pltpu.VMEM((2, 2, TOK, 2048), BF16),
            pltpu.VMEM((2, 2, TOK, 2048), BF16),
            pltpu.VMEM((2, 4, 4, 128, 512), BF16),
            pltpu.VMEM((2, TOK, 512), F32),
            pltpu.VMEM((2, 2, 2, TOK, 256), F32),
            pltpu.VMEM((2, 2, 2, TOK, 256), F32),
            pltpu.VMEM((2, 2, 5, TOK, 256), BF16),
            pltpu.VMEM((2, TOK, 2048), BF16),
            pltpu.VMEM((2, TOK, 128), F32),
            pltpu.VMEM((SLOTS, 4, 2, 4, 128, COLS), BF16),
            pltpu.VMEM((4, 6, TOK, 1024), BF16),
            pltpu.VMEM((SLOTS, 6, TOK, COLS), BF16),
            pltpu.VMEM((6 * TOK, COLS), F32),
            pltpu.VMEM((TOK, 8192), BF16),
            dma((16,)), dma((16,)),
            dma((SLOTS, 16)), dma((SLOTS, 16)),
            dma((6,)), dma((6,)),
            dma((2,)), dma((2,)),
            dma((2, 2)), dma((2, 2)),
            dma((2, 4)), dma((2, 4)),
            dma((2, 5)), dma((2, 5)),
            dma((SLOTS, 5)), dma((SLOTS, 5)),
            dma((15,)),
        ],
        compiler_params=pltpu.CompilerParams(
            collective_id=0, has_side_effects=True, vmem_limit_bytes=60 * 2 ** 20
        ),
        cost_estimate=pl.CostEstimate(flops=12 * 10 ** 9, bytes_accessed=16 * 2 ** 20, transcendentals=3 * 10 ** 6),
    )(
        lengths, hidden, queries,
        key_matrix.reshape(2, 2, 128, 512), value_matrix.reshape(2, 2, 128, 512), out_weight.reshape(2, 128, 8192),
    )
    return hidden.astype(F32) + projected.astype(F32)


def solution(mesh):
    placed = (
        P(("node", "fsdp"), None),
        P(("node", "fsdp"), None),
        P("fsdp", None),
        P("fsdp", None),
        P("fsdp", None),
        P("node", None),
    )
    return jax.shard_map(
        body, mesh=mesh, in_specs=placed, out_specs=P(("node", "fsdp"), None), check_vma=False
    )
```
